512 devices in a mesh: row: 16 (over x_lo, y, core), col: 32 (over z, x_hi).
Axes of the slice: x: 4 (x_hi: 2, x_lo: 2; x = x_hi * 2 + x_lo), y: 4, z: 16, core: 2. Of those that a mesh axis runs over, the one named last changes fastest.
Arguments:
- charges: bfloat16 [512, 8, 512], P(('row', 'col')), may hold values from -6 to 6
- dense_blocks: bfloat16 [16, 32, 4, 512, 512], P('row', 'col'), may hold values from -0.25 to 0.25
- dense_index: int32 [16, 32, 2, 4], P('row', 'col'), may hold values from 0 to 31, as said below
- dense_live: int32 [16, 32], P('row', 'col'), may hold values from 1 to 4, as said below
- left_basis: bfloat16 [16, 32, 16, 32, 512], P('row', 'col'), may hold values from -1 to 1
- right_basis: bfloat16 [16, 32, 16, 32, 512], P('row', 'col'), may hold values from -0.25 to 0.25
- low_index: int32 [16, 32, 2, 16], P('row', 'col'), may hold values from 0 to 31, as said below
Outputs:
- potential: bfloat16 [512, 8, 512], P(('row', 'col'))
The draws below stay inside these ranges and needn't reach their ends.
Inputs may be any that keep to these rules, and one draw needn't show every extreme that they name: `dense_index`: rows are local row clusters, columns local column clusters; slot 0 of each device holds the diagonal block of the cluster whose charges that device holds; pairs may repeat. `dense_live`: every device has at least 1 live slot; some device has all 4 live. `low_index`: rows are local row clusters, columns local column clusters; no admissible slot lies on the diagonal; pairs may repeat.
All inputs are finite; a program needn't handle non-finite values.
Results may differ from the reference program's by a relative error of at most 0.0049.
Values may be sent and summed in bfloat16 or wider, within the bound.
No kernel may reach another device: no remote copies, remote signals or barrier semaphores. Data moves between devices by JAX's collectives and lax.ppermute only.
A program may use at most 64 MiB of HBM per device.

```python
import jax
import jax.numpy as jnp
from jax import lax

LEAF = 512
RANK = 32
NV = 8
CL_DEV = 1
DENSE_DEV = 4
LOW_DEV = 16
ROW_GROUPS = 16
COL_GROUPS = 32
NC = 512
ROW_CL = 32
COL_CL = 16
DEVICES = 512


def group_grids(slots):
    shape = (ROW_GROUPS, COL_GROUPS, slots)
    row_group = jax.lax.broadcasted_iota(jnp.int32, shape, 0)
    col_group = jax.lax.broadcasted_iota(jnp.int32, shape, 1)
    slot = jax.lax.broadcasted_iota(jnp.int32, shape, 2)
    return (row_group, col_group, slot)


def draw_dense_index(key, part):
    key = jax.random.fold_in(key, 11)
    first, second = jax.random.split(key)
    row_group, col_group, slot = group_grids(DENSE_DEV)
    shape = (ROW_GROUPS, COL_GROUPS, DENSE_DEV)
    rows_any = jax.random.randint(first, shape, 0, ROW_CL)
    cols_any = jax.random.randint(second, shape, 0, COL_CL)
    diagonal = slot < CL_DEV
    rows = jnp.where(diagonal, col_group * CL_DEV + slot, rows_any)
    cols = jnp.where(diagonal, row_group * CL_DEV + slot, cols_any)
    return jnp.stack([rows, cols], axis=2).astype(jnp.int32)


def draw_dense_live(key, part):
    key = jax.random.fold_in(key, 23)
    keys = jax.random.split(key, 5)
    shape = (ROW_GROUPS, COL_GROUPS)
    live = jax.random.randint(keys[0], shape, CL_DEV, DENSE_DEV + 1)
    live = jnp.minimum(live, jax.random.randint(keys[1], shape, CL_DEV, DENSE_DEV + 1))
    live = jnp.minimum(live, jax.random.randint(keys[2], shape, CL_DEV, DENSE_DEV + 1))
    flat = live.reshape(-1)
    busiest = jax.random.randint(keys[3], (), 0, DEVICES)
    lightest = (busiest + 1 + jax.random.randint(keys[4], (), 0, DEVICES - 1)) % DEVICES
    flat = flat.at[busiest].set(DENSE_DEV)
    flat = flat.at[lightest].set(CL_DEV)
    return flat.reshape(shape).astype(jnp.int32)


def draw_low_index(key, part):
    key = jax.random.fold_in(key, 37)
    first, second = jax.random.split(key)
    row_group, col_group, slot = group_grids(LOW_DEV)
    shape = (ROW_GROUPS, COL_GROUPS, LOW_DEV)
    rows = jax.random.randint(first, shape, 0, ROW_CL)
    cols = jax.random.randint(second, shape, 0, COL_CL)
    row_global = row_group * ROW_CL + rows
    col_global = (cols // CL_DEV * COL_GROUPS + col_group) * CL_DEV + cols % CL_DEV
    cols = jnp.where(row_global == col_global, (cols + CL_DEV) % COL_CL, cols)
    return jnp.stack([rows, cols], axis=2).astype(jnp.int32)


def level_of(key, extent, cuts, least, high):
    def one(axis_at, parts):
        steps = jax.random.uniform(jax.random.fold_in(jax.random.fold_in(key, 6), axis_at), (parts,), jnp.float32, least / len(cuts), high / len(cuts))
        return jnp.repeat(jnp.exp(steps), extent[axis_at] // parts).reshape((-1,) + (1,) * (len(extent) - axis_at - 1))

    gain = one(*cuts[0])
    for cut in cuts[1:]:
        gain = gain * one(*cut)
    return gain


def centred(stream_key, shape, width, bound, pieces=(), held_as=jnp.bfloat16):
    array = width * jax.random.normal(stream_key, shape, jnp.float32)
    if pieces:
        array = array * level_of(stream_key, shape, pieces, -0.22, 0.18)
    return jnp.clip(array, -bound, bound).astype(held_as)


def setup_inputs(seed: int = 0) -> dict:
    arg_keys = jax.random.split(jax.random.key(seed), 8)
    return {
        "charges": centred(arg_keys[0], (NC, NV, LEAF), 1.0, 6.0, ((0, 512),)),
        "dense_blocks": centred(arg_keys[1], (ROW_GROUPS, COL_GROUPS, DENSE_DEV, LEAF, LEAF), LEAF ** -0.5, 0.25, ((0, 16), (1, 32))),
        "dense_index": draw_dense_index(jax.random.fold_in(arg_keys[7], 71), 0),
        "dense_live": draw_dense_live(jax.random.fold_in(arg_keys[7], 71), 0),
        "left_basis": centred(arg_keys[4], (ROW_GROUPS, COL_GROUPS, LOW_DEV, RANK, LEAF), RANK ** -0.5, 1.0, ((0, 16), (1, 32))),
        "right_basis": centred(arg_keys[5], (ROW_GROUPS, COL_GROUPS, LOW_DEV, RANK, LEAF), LEAF ** -0.5, 0.25, ((0, 16), (1, 32))),
        "low_index": draw_low_index(jax.random.fold_in(arg_keys[7], 71), 0),
    }


def column_cluster(local_col, col_group):
    return ((local_col // CL_DEV) * COL_GROUPS + col_group) * CL_DEV + local_col % CL_DEV


def reference(charges, dense_blocks, dense_index, dense_live, left_basis, right_basis, low_index):
    upper_bound = lax.Precision.HIGHEST
    source_vector = charges.astype(jnp.float32)
    count = ROW_GROUPS * COL_GROUPS
    flat_blocks = dense_blocks.reshape(count, DENSE_DEV, LEAF, LEAF)
    flat_dense = dense_index.reshape(count, 2, DENSE_DEV)
    flat_live = dense_live.reshape(count)
    flat_left = left_basis.reshape(count, LOW_DEV, RANK, LEAF)
    flat_right = right_basis.reshape(count, LOW_DEV, RANK, LEAF)
    flat_low = low_index.reshape(count, 2, LOW_DEV)
    device_ids = jnp.arange(count, dtype=jnp.int32)

    def step(grand_total, inputs):
        blocks, dense_pairs, live, left, right_factor_matrix, low_pairs, device = inputs
        row_group = device // COL_GROUPS
        col_group = device % COL_GROUPS
        rows_d = row_group * ROW_CL + dense_pairs[0]
        cols_d = column_cluster(dense_pairs[1], col_group)
        alive = (jnp.arange(DENSE_DEV, dtype=jnp.int32) < live).astype(jnp.float32)
        mirrored = alive * (rows_d != cols_d).astype(jnp.float32)
        block_f = blocks.astype(jnp.float32)
        forward = jnp.einsum('snl,sml->snm', source_vector[cols_d], block_f, precision=upper_bound)
        mirror = jnp.einsum('snm,sml->snl', source_vector[rows_d], block_f, precision=upper_bound)
        grand_total = grand_total.at[rows_d].add(forward * alive[:, None, None])
        grand_total = grand_total.at[cols_d].add(mirror * mirrored[:, None, None])
        row_leaves = row_group * ROW_CL + low_pairs[0]
        column_leaves = column_cluster(low_pairs[1], col_group)
        left_factor = left.astype(jnp.float32)
        right_factor = right_factor_matrix.astype(jnp.float32)
        coef_fwd = jnp.einsum('czq,cpq->czp', source_vector[column_leaves], right_factor, precision=upper_bound).astype(jnp.bfloat16).astype(jnp.float32)
        mirror_coefficient = jnp.einsum('czq,cpq->czp', source_vector[row_leaves], left_factor, precision=upper_bound).astype(jnp.bfloat16).astype(jnp.float32)
        grand_total = grand_total.at[row_leaves].add(jnp.einsum('eca,ead->ecd', coef_fwd, left_factor, precision=upper_bound))
        grand_total = grand_total.at[column_leaves].add(jnp.einsum('eca,ead->ecd', mirror_coefficient, right_factor, precision=upper_bound))
        return grand_total, None

    start = jnp.zeros((NC, NV, LEAF), jnp.float32)
    grand_total, unused = lax.scan(step, start, (flat_blocks, flat_dense, flat_live, flat_left, flat_right, flat_low, device_ids))
    return grand_total.astype(jnp.bfloat16)
```

```python
import functools

import jax
import jax.numpy as jnp
from jax import lax
from jax.experimental import pallas as pl
from jax.experimental.pallas import tpu as pltpu
from jax.sharding import PartitionSpec as P

NT = (((1,), (1,)), ((), ()))
NN = (((1,), (0,)), ((), ()))


def slot_lanes(index_ref, which, vectors, slots, rank):
    lane = lax.broadcasted_iota(jnp.int32, (vectors, slots * rank), 1)
    found = jnp.zeros(lane.shape, jnp.int32)
    for slot in range(slots):
        found = jnp.where(lane // rank == slot, index_ref[which, slot], found)
    return found


def add_up(mirror, lead, slots, rank, low_ref, dense_ref, scale_ref, charge, packed, memory, total):
    first, second, blocks, copies = memory
    source, target = (0, 1) if mirror else (1, 0)
    sources, vectors, _ = charge.shape
    targets = total.shape[0]
    source_lead, target_lead = (lead, 0) if mirror else (0, lead)
    width = slots * rank
    from_lane = slot_lanes(low_ref, source, vectors, slots, rank)
    to_lane = slot_lanes(low_ref, target, vectors, slots, rank)
    copies[0].wait()
    every = lax.dot_general(packed, first[...], NT, preferred_element_type=jnp.float32)
    every = every.reshape(sources, vectors, width)
    coef = jnp.zeros((vectors, width), jnp.float32)
    for place in range(sources):
        coef = jnp.where(from_lane == (place + source_lead) % sources, every[place], coef)
    coef = coef.astype(jnp.bfloat16).astype(jnp.float32)
    spread = [
        jnp.where(to_lane == (place + target_lead) % targets, coef, 0.0)
        for place in range(targets)
    ]
    wide = jnp.concatenate(spread, axis=0).astype(jnp.bfloat16)
    copies[1].wait()
    low = lax.dot_general(wide, second[...], NN, preferred_element_type=jnp.float32)
    total[...] = low.reshape(total.shape)
    for slot in range(blocks.shape[0]):
        copies[2 + slot].wait()
        term = lax.dot_general(
            charge[lax.rem(dense_ref[source, slot] + sources - source_lead, sources)].astype(jnp.bfloat16),
            blocks[slot],
            NN if mirror else NT,
            preferred_element_type=jnp.float32,
        )
        place = lax.rem(dense_ref[target, slot] + targets - target_lead, targets)
        total[place] = total[place] + term * scale_ref[slot]


def fetch(first_hbm, second_hbm, block_hbm, first, second, blocks, sems):
    copies = [
        pltpu.make_async_copy(first_hbm, first, sems.at[0]),
        pltpu.make_async_copy(second_hbm, second, sems.at[1]),
    ]
    for slot in range(blocks.shape[0]):
        copies.append(
            pltpu.make_async_copy(block_hbm.at[slot], blocks.at[slot], sems.at[2 + slot])
        )
    for copy in copies:
        copy.start()
    return first, second, blocks, copies


def forward_kernel(
    lead, slots, rank,
    low_ref, dense_ref, scale_ref, charge_ref, own_ref, first_hbm, second_hbm, block_hbm, out_ref,
    first, second, blocks, charge, total, sems,
):
    memory = fetch(first_hbm, second_hbm, block_hbm, first, second, blocks, sems)
    packed = charge_ref[...]
    charge[...] = packed.astype(jnp.float32).reshape(charge.shape)
    add_up(False, lead, slots, rank, low_ref, dense_ref, scale_ref, charge, packed, memory, total)
    own = jnp.broadcast_to(own_ref[...].astype(jnp.float32), total.shape)
    out_ref[...] = jnp.concatenate([total[...], own], axis=1).astype(out_ref.dtype)


def mirror_kernel(
    lead, slots, rank,
    low_ref, dense_ref, scale_ref, mixed_ref, first_hbm, second_hbm, block_hbm, out_ref, sum_ref,
    first, second, blocks, charge, total, sems,
):
    memory = fetch(first_hbm, second_hbm, block_hbm, first, second, blocks, sems)
    vectors = charge.shape[1]
    mixed = mixed_ref[...].astype(jnp.float32)
    charge[...] = mixed[:, vectors:]
    sum_ref[...] = jnp.sum(mixed[:, :vectors], axis=0)
    packed = charge[...].reshape(-1, charge.shape[2]).astype(jnp.bfloat16)
    add_up(True, lead, slots, rank, low_ref, dense_ref, scale_ref, charge, packed, memory, total)
    out_ref[...] = total[...].reshape(out_ref.shape).astype(out_ref.dtype)


def apply_slots(kernel, lead, room, pairs, arrays, bases, blocks, sources, targets, out_shape):
    slots, rank, leaf = bases[0].shape
    vectors = 8
    flat = slots * rank
    smem = pl.BlockSpec(memory_space=pltpu.SMEM)
    vmem = pl.BlockSpec(memory_space=pltpu.VMEM)
    anywhere = pl.BlockSpec(memory_space=pl.ANY)
    return pl.pallas_call(
        functools.partial(kernel, lead, slots, rank),
        out_shape=out_shape,
        in_specs=[smem] * 3 + [vmem] * len(arrays) + [anywhere] * 3,
        out_specs=jax.tree.map(lambda _: vmem, out_shape),
        scratch_shapes=[
            pltpu.VMEM((flat, leaf), jnp.bfloat16),
            pltpu.VMEM((flat, leaf), jnp.bfloat16),
            pltpu.VMEM(blocks.shape, jnp.bfloat16),
            pltpu.VMEM((sources, vectors, leaf), jnp.float32),
            pltpu.VMEM((targets, vectors, leaf), jnp.float32),
            pltpu.SemaphoreType.DMA((2 + blocks.shape[0],)),
        ],
        compiler_params=pltpu.CompilerParams(vmem_limit_bytes=room * 1024 * 1024),
        cost_estimate=pl.CostEstimate(
            flops=2 * leaf * flat * vectors * (sources + targets + blocks.shape[0]),
            bytes_accessed=2 * (2 * flat * leaf + blocks.size),
            transcendentals=0,
        ),
    )(*pairs, *arrays, *[basis.reshape(flat, leaf) for basis in bases], blocks)


def on_device(charges, dense_blocks, dense_index, dense_live, left_basis, right_basis, low_index):
    _, vectors, leaf = charges.shape
    rows = lax.axis_size("col")
    cols = lax.axis_size("row")
    lead = rows // 2
    order = [(place + lead) % rows for place in range(rows)]
    copies = jnp.broadcast_to(charges, (cols, vectors, leaf))
    col_charges = lax.all_to_all(copies, "row", 0, 0, tiled=True)
    blocks = dense_blocks[0, 0]
    dense_pairs = dense_index[0, 0]
    left = left_basis[0, 0]
    right = right_basis[0, 0]
    low_pairs = low_index[0, 0]
    alive = jnp.arange(blocks.shape[0], dtype=jnp.int32) < dense_live[0, 0]
    diagonal = (dense_pairs[0] == lax.axis_index("col")) & (dense_pairs[1] == lax.axis_index("row"))
    forward_scale = alive.astype(jnp.float32)
    mirror_scale = (alive & ~diagonal).astype(jnp.float32)
    mixed = apply_slots(
        forward_kernel, lead, 60,
        (low_pairs, dense_pairs, forward_scale),
        (col_charges.reshape(cols * vectors, leaf), charges[0]),
        (right, left), blocks, cols, rows,
        jax.ShapeDtypeStruct((rows, 2 * vectors, leaf), jnp.bfloat16),
    )
    mixed = lax.all_to_all(mixed, "col", 0, 0, axis_index_groups=[order], tiled=True)
    col_partial, row_total = apply_slots(
        mirror_kernel, lead, 16,
        (low_pairs, dense_pairs, mirror_scale),
        (mixed,),
        (left, right), blocks, rows, cols,
        (
            jax.ShapeDtypeStruct((cols * vectors, leaf), jnp.bfloat16),
            jax.ShapeDtypeStruct((vectors, leaf), jnp.float32),
        ),
    )
    col_parts = lax.all_to_all(col_partial.reshape(cols, vectors, leaf), "row", 0, 0, tiled=True)
    col_total = jnp.sum(col_parts.astype(jnp.float32), axis=0)
    return (row_total + col_total).astype(jnp.bfloat16)[None]


def solution(mesh):
    in_specs = (
        P(("row", "col"), None, None),
        P("row", "col", None, None, None),
        P("row", "col", None, None),
        P("row", "col"),
        P("row", "col", None, None, None),
        P("row", "col", None, None, None),
        P("row", "col", None, None),
    )
    out_specs = P(("row", "col"), None, None)
    return jax.shard_map(
        on_device, mesh=mesh, in_specs=in_specs, out_specs=out_specs, check_vma=False
    )
```

```python
import functools

import jax
import jax.numpy as jnp
from jax import lax
from jax.experimental import pallas as pl
from jax.experimental.pallas import tpu as pltpu
from jax.sharding import PartitionSpec as P

NT = (((1,), (1,)), ((), ()))
NN = (((1,), (0,)), ((), ()))


def slot_lanes(index_ref, which, vectors, slots, rank):
    lane = lax.broadcasted_iota(jnp.int32, (vectors, slots * rank), 1)
    found = jnp.zeros(lane.shape, jnp.int32)
    for slot in range(slots):
        found = jnp.where(lane // rank == slot, index_ref[which, slot], found)
    return found


def add_up(mirror, lead, slots, rank, low_ref, dense_ref, live_ref, charge, packed, memory, total):
    first, second, blocks = memory
    source, target = (0, 1) if mirror else (1, 0)
    sources, vectors, _ = charge.shape
    targets = total.shape[0]
    source_lead, target_lead = lead
    width = slots * rank
    from_lane = slot_lanes(low_ref, source, vectors, slots, rank)
    to_lane = slot_lanes(low_ref, target, vectors, slots, rank)
    every = lax.dot_general(packed, first[...], NT, preferred_element_type=jnp.float32)
    every = every.reshape(sources, vectors, width)
    coef = jnp.zeros((vectors, width), jnp.float32)
    for place in range(sources):
        coef = jnp.where(from_lane == (place + source_lead) % sources, every[place], coef)
    coef = coef.astype(jnp.bfloat16).astype(jnp.float32)
    spread = [
        jnp.where(to_lane == (place + target_lead) % targets, coef, 0.0)
        for place in range(targets)
    ]
    wide = jnp.concatenate(spread, axis=0).astype(jnp.bfloat16)
    low = lax.dot_general(wide, second[...], NN, preferred_element_type=jnp.float32)
    total[...] = low.reshape(total.shape)
    for slot in range(blocks.shape[0]):
        alive = slot < live_ref[0, 0]
        if mirror:
            own_row = dense_ref[0, slot] == lax.axis_index("col")
            own_col = dense_ref[1, slot] == lax.axis_index("row")
            alive = alive & ~(own_row & own_col)
        scale = jnp.where(alive, 1.0, 0.0)
        term = lax.dot_general(
            charge[lax.rem(dense_ref[source, slot] + sources - source_lead, sources)].astype(jnp.bfloat16),
            blocks[slot],
            NN if mirror else NT,
            preferred_element_type=jnp.float32,
        )
        place = lax.rem(dense_ref[target, slot] + targets - target_lead, targets)
        total[place] = total[place] + term * scale


def forward_kernel(
    lead, slots, rank,
    low_ref, dense_ref, live_ref, charge_ref, own_ref, first, second, blocks, out_ref,
    charge, total,
):
    memory = (first, second, blocks)
    packed = charge_ref[...]
    charge[...] = packed.astype(jnp.float32).reshape(charge.shape)
    add_up(False, lead, slots, rank, low_ref, dense_ref, live_ref, charge, packed, memory, total)
    own = jnp.broadcast_to(own_ref[...].astype(jnp.float32), total.shape)
    out_ref[...] = jnp.concatenate([total[...], own], axis=1).astype(out_ref.dtype)


def mirror_kernel(
    lead, slots, rank,
    low_ref, dense_ref, live_ref, mixed_ref, first, second, blocks, out_ref, sum_ref,
    charge, total,
):
    memory = (first, second, blocks)
    vectors = charge.shape[1]
    mixed = mixed_ref[...].astype(jnp.float32)
    charge[...] = mixed[:, vectors:]
    sum_ref[...] = jnp.sum(mixed[:, :vectors], axis=0)
    packed = charge[...].reshape(-1, charge.shape[2]).astype(jnp.bfloat16)
    add_up(True, lead, slots, rank, low_ref, dense_ref, live_ref, charge, packed, memory, total)
    out_ref[...] = total[...].reshape(out_ref.shape).astype(out_ref.dtype)


def apply_slots(kernel, lead, room, pairs, arrays, bases, blocks, sources, targets, out_shape):
    slots, rank, leaf = bases[0].shape
    vectors = 8
    flat = slots * rank
    smem = pl.BlockSpec(memory_space=pltpu.SMEM)
    vmem = pl.BlockSpec(memory_space=pltpu.VMEM)
    return pl.pallas_call(
        functools.partial(kernel, lead, slots, rank),
        out_shape=out_shape,
        in_specs=[smem] * 3 + [vmem] * (len(arrays) + 3),
        out_specs=jax.tree.map(lambda _: vmem, out_shape),
        scratch_shapes=[
            pltpu.VMEM((sources, vectors, leaf), jnp.float32),
            pltpu.VMEM((targets, vectors, leaf), jnp.float32),
        ],
        compiler_params=pltpu.CompilerParams(vmem_limit_bytes=room * 1024 * 1024),
        cost_estimate=pl.CostEstimate(
            flops=2 * leaf * flat * vectors * (sources + targets + blocks.shape[0]),
            bytes_accessed=2 * (2 * flat * leaf + blocks.size),
            transcendentals=0,
        ),
    )(*pairs, *arrays, *[basis.reshape(flat, leaf) for basis in bases], blocks)


def hold_kernel(first_in, second_in, third_in, first_out, second_out, third_out, sems):
    copies = [
        pltpu.make_async_copy(first_in, first_out, sems.at[0]),
        pltpu.make_async_copy(second_in, second_out, sems.at[1]),
        pltpu.make_async_copy(third_in, third_out, sems.at[2]),
    ]
    for copy in copies:
        copy.start()
    for copy in copies:
        copy.wait()


def hold(*arrays):
    anywhere = pl.BlockSpec(memory_space=pl.ANY)
    return pl.pallas_call(
        hold_kernel,
        out_shape=[jax.ShapeDtypeStruct(a.shape, a.dtype) for a in arrays],
        in_specs=[anywhere] * 3,
        out_specs=[anywhere] * 3,
        scratch_shapes=[pltpu.SemaphoreType.DMA((3,))],
        compiler_params=pltpu.CompilerParams(vmem_limit_bytes=16 * 1024 * 1024),
        cost_estimate=pl.CostEstimate(
            flops=0, bytes_accessed=4 * sum(a.size for a in arrays), transcendentals=0
        ),
    )(*arrays)


def on_device(charges, dense_blocks, dense_index, dense_live, left_basis, right_basis, low_index):
    _, vectors, leaf = charges.shape
    rows = lax.axis_size("col")
    cols = lax.axis_size("row")
    col_lead = rows // 2
    col_order = [(place + col_lead) % rows for place in range(rows)]
    row_lead = cols - 2
    row_order = [(place + row_lead) % cols for place in range(cols)]
    copies = jnp.broadcast_to(charges, (cols, vectors, leaf))
    col_charges = lax.all_to_all(copies, "row", 0, 0, axis_index_groups=[row_order], tiled=True)
    left, right, blocks = hold(left_basis[0, 0], right_basis[0, 0], dense_blocks[0, 0])
    dense_pairs = dense_index[0, 0]
    low_pairs = low_index[0, 0]
    mixed = apply_slots(
        forward_kernel, (row_lead, col_lead), 16,
        (low_pairs, dense_pairs, dense_live),
        (col_charges.reshape(cols * vectors, leaf), charges[0]),
        (right, left), blocks, cols, rows,
        jax.ShapeDtypeStruct((rows, 2 * vectors, leaf), jnp.bfloat16),
    )
    mixed = lax.all_to_all(mixed, "col", 0, 0, axis_index_groups=[col_order], tiled=True)
    col_partial, row_total = apply_slots(
        mirror_kernel, (col_lead, 0), 16,
        (low_pairs, dense_pairs, dense_live),
        (mixed,),
        (left, right), blocks, rows, cols,
        (
            jax.ShapeDtypeStruct((cols * vectors, leaf), jnp.bfloat16),
            jax.ShapeDtypeStruct((vectors, leaf), jnp.float32),
        ),
    )
    col_parts = lax.all_to_all(col_partial.reshape(cols, vectors, leaf), "row", 0, 0, tiled=True)
    col_total = jnp.sum(col_parts.astype(jnp.float32), axis=0)
    return (row_total + col_total).astype(jnp.bfloat16)[None]


def solution(mesh):
    in_specs = (
        P(("row", "col"), None, None),
        P("row", "col", None, None, None),
        P("row", "col", None, None),
        P("row", "col"),
        P("row", "col", None, None, None),
        P("row", "col", None, None, None),
        P("row", "col", None, None),
    )
    out_specs = P(("row", "col"), None, None)
    return jax.shard_map(
        on_device, mesh=mesh, in_specs=in_specs, out_specs=out_specs, check_vma=False
    )
```

```python
import functools

import jax
import jax.numpy as jnp
from jax import lax
from jax.experimental import pallas as pl
from jax.experimental.pallas import tpu as pltpu
from jax.sharding import PartitionSpec as P

NT = (((1,), (1,)), ((), ()))
NN = (((1,), (0,)), ((), ()))


def turned(count, lead):
    order = [(place + lead) % count for place in range(count)]
    return order, lambda index: lax.rem(index + (count - lead), count)


def outward(count, centre):
    pairs = count // 2
    steps = [0]
    for step in range(1, pairs // 2 + 1):
        steps += [step, -step]
    steps = steps[:pairs]
    order = [2 * ((centre + step) % pairs) + half for step in steps for half in (0, 1)]

    def place(index):
        step = lax.rem(lax.div(index, 2) + (pairs - centre), pairs)
        ahead = (step >= 1) & (step <= pairs // 2)
        pair = jnp.where(ahead, 2 * step - 1, lax.rem(2 * (pairs - step), 2 * pairs))
        return 2 * pair + lax.rem(index, 2)

    return order, place


def slot_lanes(index_ref, which, vectors, slots, rank):
    lane = lax.broadcasted_iota(jnp.int32, (vectors, slots * rank), 1)
    found = jnp.zeros(lane.shape, jnp.int32)
    for slot in range(slots):
        found = jnp.where(lane // rank == slot, index_ref[which, slot], found)
    return found


def add_up(mirror, lines, slots, rank, low_ref, dense_ref, live_ref, charge, packed, memory, total):
    first, second, blocks = memory
    source, target = (0, 1) if mirror else (1, 0)
    sources, vectors, _ = charge.shape
    targets = total.shape[0]
    (source_order, source_place), (target_order, target_place) = lines
    width = slots * rank
    from_lane = slot_lanes(low_ref, source, vectors, slots, rank)
    to_lane = slot_lanes(low_ref, target, vectors, slots, rank)
    every = lax.dot_general(packed, first[...], NT, preferred_element_type=jnp.float32)
    every = every.reshape(sources, vectors, width)
    coef = jnp.zeros((vectors, width), jnp.float32)
    for place, cluster in enumerate(source_order):
        coef = jnp.where(from_lane == cluster, every[place], coef)
    coef = coef.astype(jnp.bfloat16).astype(jnp.float32)
    spread = [jnp.where(to_lane == cluster, coef, 0.0) for cluster in target_order]
    wide = jnp.concatenate(spread, axis=0).astype(jnp.bfloat16)
    low = lax.dot_general(wide, second[...], NN, preferred_element_type=jnp.float32)
    total[...] = low.reshape(total.shape)
    for slot in range(blocks.shape[0]):
        alive = slot < live_ref[0, 0]
        if mirror:
            own_row = dense_ref[0, slot] == lax.axis_index("col")
            own_col = dense_ref[1, slot] == lax.axis_index("row")
            alive = alive & ~(own_row & own_col)
        scale = jnp.where(alive, 1.0, 0.0)
        term = lax.dot_general(
            charge[source_place(dense_ref[source, slot])].astype(jnp.bfloat16),
            blocks[slot],
            NN if mirror else NT,
            preferred_element_type=jnp.float32,
        )
        place = target_place(dense_ref[target, slot])
        total[place] = total[place] + term * scale


def forward_kernel(
    lines, slots, rank,
    low_ref, dense_ref, live_ref, charge_ref, own_ref, first, second, blocks, out_ref,
    charge, total,
):
    memory = (first, second, blocks)
    packed = charge_ref[...]
    charge[...] = packed.astype(jnp.float32).reshape(charge.shape)
    add_up(False, lines, slots, rank, low_ref, dense_ref, live_ref, charge, packed, memory, total)
    own = jnp.broadcast_to(own_ref[...].astype(jnp.float32), total.shape)
    out_ref[...] = jnp.concatenate([total[...], own], axis=1).astype(out_ref.dtype)


def mirror_kernel(
    lines, slots, rank,
    low_ref, dense_ref, live_ref, mixed_ref, first, second, blocks, out_ref, sum_ref,
    charge, total,
):
    memory = (first, second, blocks)
    vectors = charge.shape[1]
    mixed = mixed_ref[...].astype(jnp.float32)
    charge[...] = mixed[:, vectors:]
    sum_ref[...] = jnp.sum(mixed[:, :vectors], axis=0)
    packed = charge[...].reshape(-1, charge.shape[2]).astype(jnp.bfloat16)
    add_up(True, lines, slots, rank, low_ref, dense_ref, live_ref, charge, packed, memory, total)
    out_ref[...] = total[...].reshape(out_ref.shape).astype(out_ref.dtype)


def apply_slots(kernel, lines, room, pairs, arrays, bases, blocks, sources, targets, out_shape):
    slots, rank, leaf = bases[0].shape
    vectors = 8
    flat = slots * rank
    smem = pl.BlockSpec(memory_space=pltpu.SMEM)
    vmem = pl.BlockSpec(memory_space=pltpu.VMEM)
    return pl.pallas_call(
        functools.partial(kernel, lines, slots, rank),
        out_shape=out_shape,
        in_specs=[smem] * 3 + [vmem] * (len(arrays) + 3),
        out_specs=jax.tree.map(lambda _: vmem, out_shape),
        scratch_shapes=[
            pltpu.VMEM((sources, vectors, leaf), jnp.float32),
            pltpu.VMEM((targets, vectors, leaf), jnp.float32),
        ],
        compiler_params=pltpu.CompilerParams(vmem_limit_bytes=room * 1024 * 1024),
        cost_estimate=pl.CostEstimate(
            flops=2 * leaf * flat * vectors * (sources + targets + blocks.shape[0]),
            bytes_accessed=2 * (2 * flat * leaf + blocks.size),
            transcendentals=0,
        ),
    )(*pairs, *arrays, *[basis.reshape(flat, leaf) for basis in bases], blocks)


def hold_kernel(first_in, second_in, third_in, first_out, second_out, third_out, sems):
    copies = [
        pltpu.make_async_copy(first_in, first_out, sems.at[0]),
        pltpu.make_async_copy(second_in, second_out, sems.at[1]),
        pltpu.make_async_copy(third_in, third_out, sems.at[2]),
    ]
    for copy in copies:
        copy.start()
    for copy in copies:
        copy.wait()


def hold(*arrays):
    anywhere = pl.BlockSpec(memory_space=pl.ANY)
    return pl.pallas_call(
        hold_kernel,
        out_shape=[jax.ShapeDtypeStruct(a.shape, a.dtype) for a in arrays],
        in_specs=[anywhere] * 3,
        out_specs=[anywhere] * 3,
        scratch_shapes=[pltpu.SemaphoreType.DMA((3,))],
        compiler_params=pltpu.CompilerParams(vmem_limit_bytes=16 * 1024 * 1024),
        cost_estimate=pl.CostEstimate(
            flops=0, bytes_accessed=4 * sum(a.size for a in arrays), transcendentals=0
        ),
    )(*arrays)


def on_device(charges, dense_blocks, dense_index, dense_live, left_basis, right_basis, low_index):
    _, vectors, leaf = charges.shape
    rows = lax.axis_size("col")
    cols = lax.axis_size("row")
    row_line = turned(cols, cols - 2)
    col_line = outward(rows, 10)
    copies = jnp.broadcast_to(charges, (cols, vectors, leaf))
    col_charges = lax.all_to_all(copies, "row", 0, 0, axis_index_groups=[row_line[0]], tiled=True)
    left, right, blocks = hold(left_basis[0, 0], right_basis[0, 0], dense_blocks[0, 0])
    dense_pairs = dense_index[0, 0]
    low_pairs = low_index[0, 0]
    mixed = apply_slots(
        forward_kernel, (row_line, col_line), 16,
        (low_pairs, dense_pairs, dense_live),
        (col_charges.reshape(cols * vectors, leaf), charges[0]),
        (right, left), blocks, cols, rows,
        jax.ShapeDtypeStruct((rows, 2 * vectors, leaf), jnp.bfloat16),
    )
    mixed = lax.all_to_all(mixed, "col", 0, 0, axis_index_groups=[col_line[0]], tiled=True)
    col_partial, row_total = apply_slots(
        mirror_kernel, (col_line, turned(cols, 0)), 16,
        (low_pairs, dense_pairs, dense_live),
        (mixed,),
        (left, right), blocks, rows, cols,
        (
            jax.ShapeDtypeStruct((cols * vectors, leaf), jnp.bfloat16),
            jax.ShapeDtypeStruct((vectors, leaf), jnp.float32),
        ),
    )
    col_parts = lax.all_to_all(col_partial.reshape(cols, vectors, leaf), "row", 0, 0, tiled=True)
    col_total = jnp.sum(col_parts.astype(jnp.float32), axis=0)
    return (row_total + col_total).astype(jnp.bfloat16)[None]


def solution(mesh):
    in_specs = (
        P(("row", "col"), None, None),
        P("row", "col", None, None, None),
        P("row", "col", None, None),
        P("row", "col"),
        P("row", "col", None, None, None),
        P("row", "col", None, None, None),
        P("row", "col", None, None),
    )
    out_specs = P(("row", "col"), None, None)
    return jax.shard_map(
        on_device, mesh=mesh, in_specs=in_specs, out_specs=out_specs, check_vma=False
    )
```

```python
import functools

import jax
import jax.numpy as jnp
from jax import lax
from jax.experimental import pallas as pl
from jax.experimental.pallas import tpu as pltpu
from jax.sharding import PartitionSpec as P

NT = (((1,), (1,)), ((), ()))
NN = (((1,), (0,)), ((), ()))


def turned(count, lead):
    order = [(place + lead) % count for place in range(count)]
    return order, lambda index: lax.rem(index + (count - lead), count)


def outward(count, centre):
    pairs = count // 2
    steps = [0]
    for step in range(1, pairs // 2 + 1):
        steps += [step, -step]
    steps = steps[:pairs]
    order = [2 * ((centre + step) % pairs) + half for step in steps for half in (0, 1)]

    def place(index):
        step = lax.rem(lax.div(index, 2) + (pairs - centre), pairs)
        ahead = (step >= 1) & (step <= pairs // 2)
        pair = jnp.where(ahead, 2 * step - 1, lax.rem(2 * (pairs - step), 2 * pairs))
        return 2 * pair + lax.rem(index, 2)

    return order, place


def slot_lanes(index_ref, which, vectors, slots, rank):
    lane = lax.broadcasted_iota(jnp.int32, (vectors, slots * rank), 1)
    found = jnp.zeros(lane.shape, jnp.int32)
    for slot in range(slots):
        found = jnp.where(lane // rank == slot, index_ref[which, slot], found)
    return found


def add_up(mirror, lines, slots, rank, low_ref, dense_ref, live_ref, charge, packed, memory, total):
    first, second, blocks = memory
    source, target = (0, 1) if mirror else (1, 0)
    sources, vectors, _ = charge.shape
    targets = total.shape[0]
    (source_order, source_place), (target_order, target_place) = lines
    width = slots * rank
    from_lane = slot_lanes(low_ref, source, vectors, slots, rank)
    to_lane = slot_lanes(low_ref, target, vectors, slots, rank)
    every = lax.dot_general(packed, first[...], NT, preferred_element_type=jnp.float32)
    every = every.reshape(sources, vectors, width)
    coef = jnp.zeros((vectors, width), jnp.float32)
    for place, cluster in enumerate(source_order):
        coef = jnp.where(from_lane == cluster, every[place], coef)
    coef = coef.astype(jnp.bfloat16).astype(jnp.float32)
    spread = [jnp.where(to_lane == cluster, coef, 0.0) for cluster in target_order]
    wide = jnp.concatenate(spread, axis=0).astype(jnp.bfloat16)
    low = lax.dot_general(wide, second[...], NN, preferred_element_type=jnp.float32)
    total[...] = low.reshape(total.shape)
    for slot in range(blocks.shape[0]):
        alive = slot < live_ref[0, 0]
        if mirror:
            own_row = dense_ref[0, slot] == lax.axis_index("col")
            own_col = dense_ref[1, slot] == lax.axis_index("row")
            alive = alive & ~(own_row & own_col)
        scale = jnp.where(alive, 1.0, 0.0)
        term = lax.dot_general(
            charge[source_place(dense_ref[source, slot])].astype(jnp.bfloat16),
            blocks[slot],
            NN if mirror else NT,
            preferred_element_type=jnp.float32,
        )
        place = target_place(dense_ref[target, slot])
        total[place] = total[place] + term * scale


def forward_kernel(
    lines, slots, rank,
    low_ref, dense_ref, live_ref, charge_ref, own_ref, first, second, blocks, out_ref,
    charge, total,
):
    memory = (first, second, blocks)
    packed = charge_ref[...]
    charge[...] = packed.astype(jnp.float32).reshape(charge.shape)
    add_up(False, lines, slots, rank, low_ref, dense_ref, live_ref, charge, packed, memory, total)
    own = jnp.broadcast_to(own_ref[...].astype(jnp.float32), total.shape)
    out_ref[...] = jnp.concatenate([total[...], own], axis=1).astype(out_ref.dtype)


def mirror_kernel(
    lines, slots, rank,
    low_ref, dense_ref, live_ref, mixed_ref, first, second, blocks, out_ref, sum_ref,
    charge, total,
):
    memory = (first, second, blocks)
    vectors = charge.shape[1]
    mixed = mixed_ref[...].astype(jnp.float32)
    charge[...] = mixed[:, vectors:]
    sum_ref[...] = jnp.sum(mixed[:, :vectors], axis=0)
    packed = charge[...].reshape(-1, charge.shape[2]).astype(jnp.bfloat16)
    add_up(True, lines, slots, rank, low_ref, dense_ref, live_ref, charge, packed, memory, total)
    out_ref[...] = total[...].reshape(out_ref.shape).astype(out_ref.dtype)


def apply_slots(kernel, lines, room, pairs, arrays, bases, blocks, sources, targets, out_shape):
    slots, rank, leaf = bases[0].shape
    vectors = 8
    flat = slots * rank
    smem = pl.BlockSpec(memory_space=pltpu.SMEM)
    vmem = pl.BlockSpec(memory_space=pltpu.VMEM)
    return pl.pallas_call(
        functools.partial(kernel, lines, slots, rank),
        out_shape=out_shape,
        in_specs=[smem] * 3 + [vmem] * (len(arrays) + 3),
        out_specs=jax.tree.map(lambda _: vmem, out_shape),
        scratch_shapes=[
            pltpu.VMEM((sources, vectors, leaf), jnp.float32),
            pltpu.VMEM((targets, vectors, leaf), jnp.float32),
        ],
        compiler_params=pltpu.CompilerParams(vmem_limit_bytes=room * 1024 * 1024),
        cost_estimate=pl.CostEstimate(
            flops=2 * leaf * flat * vectors * (sources + targets + blocks.shape[0]),
            bytes_accessed=2 * (2 * flat * leaf + blocks.size),
            transcendentals=0,
        ),
    )(*pairs, *arrays, *[basis.reshape(flat, leaf) for basis in bases], blocks)


def hold_kernel(first_in, second_in, third_in, first_out, second_out, third_out, sems):
    copies = [
        pltpu.make_async_copy(first_in, first_out, sems.at[0]),
        pltpu.make_async_copy(second_in, second_out, sems.at[1]),
        pltpu.make_async_copy(third_in, third_out, sems.at[2]),
    ]
    for copy in copies:
        copy.start()
    for copy in copies:
        copy.wait()


def hold(*arrays):
    anywhere = pl.BlockSpec(memory_space=pl.ANY)
    return pl.pallas_call(
        hold_kernel,
        out_shape=[jax.ShapeDtypeStruct(a.shape, a.dtype) for a in arrays],
        in_specs=[anywhere] * 3,
        out_specs=[anywhere] * 3,
        scratch_shapes=[pltpu.SemaphoreType.DMA((3,))],
        compiler_params=pltpu.CompilerParams(vmem_limit_bytes=16 * 1024 * 1024),
        cost_estimate=pl.CostEstimate(
            flops=0, bytes_accessed=4 * sum(a.size for a in arrays), transcendentals=0
        ),
    )(*arrays)


def on_device(charges, dense_blocks, dense_index, dense_live, left_basis, right_basis, low_index):
    _, vectors, leaf = charges.shape
    rows = lax.axis_size("col")
    cols = lax.axis_size("row")
    row_line = turned(cols, cols - 2)
    back_line = turned(cols, 4)
    col_line = outward(rows, 10)
    copies = jnp.broadcast_to(charges, (cols, vectors, leaf))
    col_charges = lax.all_to_all(copies, "row", 0, 0, axis_index_groups=[row_line[0]], tiled=True)
    left, right, blocks = hold(left_basis[0, 0], right_basis[0, 0], dense_blocks[0, 0])
    dense_pairs = dense_index[0, 0]
    low_pairs = low_index[0, 0]
    mixed = apply_slots(
        forward_kernel, (row_line, col_line), 16,
        (low_pairs, dense_pairs, dense_live),
        (col_charges.reshape(cols * vectors, leaf), charges[0]),
        (right, left), blocks, cols, rows,
        jax.ShapeDtypeStruct((rows, 2 * vectors, leaf), jnp.bfloat16),
    )
    mixed = lax.all_to_all(mixed, "col", 0, 0, axis_index_groups=[col_line[0]], tiled=True)
    col_partial, row_total = apply_slots(
        mirror_kernel, (col_line, back_line), 16,
        (low_pairs, dense_pairs, dense_live),
        (mixed,),
        (left, right), blocks, rows, cols,
        (
            jax.ShapeDtypeStruct((cols * vectors, leaf), jnp.bfloat16),
            jax.ShapeDtypeStruct((vectors, leaf), jnp.float32),
        ),
    )
    col_parts = lax.all_to_all(
        col_partial.reshape(cols, vectors, leaf), "row", 0, 0,
        axis_index_groups=[back_line[0]], tiled=True,
    )
    col_total = jnp.sum(col_parts.astype(jnp.float32), axis=0)
    return (row_total + col_total).astype(jnp.bfloat16)[None]


def solution(mesh):
    in_specs = (
        P(("row", "col"), None, None),
        P("row", "col", None, None, None),
        P("row", "col", None, None),
        P("row", "col"),
        P("row", "col", None, None, None),
        P("row", "col", None, None, None),
        P("row", "col", None, None),
    )
    out_specs = P(("row", "col"), None, None)
    return jax.shard_map(
        on_device, mesh=mesh, in_specs=in_specs, out_specs=out_specs, check_vma=False
    )
```

```python
import functools

import jax
import jax.numpy as jnp
from jax import lax
from jax.experimental import pallas as pl
from jax.experimental.pallas import tpu as pltpu
from jax.sharding import PartitionSpec as P

NT = (((1,), (1,)), ((), ()))
NN = (((1,), (0,)), ((), ()))


def turned(count, lead):
    order = [(place + lead) % count for place in range(count)]
    return order, lambda index: lax.rem(index + (count - lead), count)


def outward(count, centre):
    pairs = count // 2
    steps = [0]
    for step in range(1, pairs // 2 + 1):
        steps += [step, -step]
    steps = steps[:pairs]
    order = [2 * ((centre + step) % pairs) + half for step in steps for half in (0, 1)]

    def place(index):
        step = lax.rem(lax.div(index, 2) + (pairs - centre), pairs)
        ahead = (step >= 1) & (step <= pairs // 2)
        pair = jnp.where(ahead, 2 * step - 1, lax.rem(2 * (pairs - step), 2 * pairs))
        return 2 * pair + lax.rem(index, 2)

    return order, place


def slot_lanes(index_ref, which, vectors, slots, rank):
    lane = lax.broadcasted_iota(jnp.int32, (vectors, slots * rank), 1)
    found = jnp.zeros(lane.shape, jnp.int32)
    for slot in range(slots):
        found = jnp.where(lane // rank == slot, index_ref[which, slot], found)
    return found


def add_up(mirror, lines, slots, rank, low_ref, dense_ref, live_ref, charge, packed, memory, total):
    first, second, blocks = memory
    source, target = (0, 1) if mirror else (1, 0)
    sources, vectors, _ = charge.shape
    targets = total.shape[0]
    (source_order, source_place), (target_order, target_place) = lines
    width = slots * rank
    from_lane = slot_lanes(low_ref, source, vectors, slots, rank)
    to_lane = slot_lanes(low_ref, target, vectors, slots, rank)
    every = lax.dot_general(packed, first[...], NT, preferred_element_type=jnp.float32)
    every = every.reshape(sources, vectors, width)
    coef = jnp.zeros((vectors, width), jnp.float32)
    for place, cluster in enumerate(source_order):
        coef = jnp.where(from_lane == cluster, every[place], coef)
    coef = coef.astype(jnp.bfloat16).astype(jnp.float32)
    spread = [jnp.where(to_lane == cluster, coef, 0.0) for cluster in target_order]
    wide = jnp.concatenate(spread, axis=0).astype(jnp.bfloat16)
    low = lax.dot_general(wide, second[...], NN, preferred_element_type=jnp.float32)
    total[...] = low.reshape(total.shape)
    for slot in range(blocks.shape[0]):
        alive = slot < live_ref[0, 0]
        if mirror:
            own_row = dense_ref[0, slot] == lax.axis_index("col")
            own_col = dense_ref[1, slot] == lax.axis_index("row")
            alive = alive & ~(own_row & own_col)
        scale = jnp.where(alive, 1.0, 0.0)
        term = lax.dot_general(
            charge[source_place(dense_ref[source, slot])].astype(jnp.bfloat16),
            blocks[slot],
            NN if mirror else NT,
            preferred_element_type=jnp.float32,
        )
        place = target_place(dense_ref[target, slot])
        total[place] = total[place] + term * scale


def forward_kernel(
    lines, slots, rank,
    low_ref, dense_ref, live_ref, charge_ref, own_ref, first, second, blocks, out_ref,
    charge, total,
):
    memory = (first, second, blocks)
    packed = charge_ref[...]
    charge[...] = packed.astype(jnp.float32).reshape(charge.shape)
    add_up(False, lines, slots, rank, low_ref, dense_ref, live_ref, charge, packed, memory, total)
    own = jnp.broadcast_to(own_ref[...].astype(jnp.float32), total.shape)
    out_ref[...] = jnp.concatenate([total[...], own], axis=1).astype(out_ref.dtype)


def mirror_kernel(
    lines, slots, rank,
    low_ref, dense_ref, live_ref, mixed_ref, first, second, blocks, out_ref, sum_ref,
    charge, total,
):
    memory = (first, second, blocks)
    vectors = charge.shape[1]
    mixed = mixed_ref[...].astype(jnp.float32)
    charge[...] = mixed[:, vectors:]
    sum_ref[...] = jnp.sum(mixed[:, :vectors], axis=0)
    packed = charge[...].reshape(-1, charge.shape[2]).astype(jnp.bfloat16)
    add_up(True, lines, slots, rank, low_ref, dense_ref, live_ref, charge, packed, memory, total)
    out_ref[...] = total[...].reshape(out_ref.shape).astype(out_ref.dtype)


def apply_slots(kernel, lines, room, pairs, arrays, bases, blocks, sources, targets, out_shape):
    slots, rank, leaf = bases[0].shape
    vectors = 8
    flat = slots * rank
    smem = pl.BlockSpec(memory_space=pltpu.SMEM)
    vmem = pl.BlockSpec(memory_space=pltpu.VMEM)
    return pl.pallas_call(
        functools.partial(kernel, lines, slots, rank),
        out_shape=out_shape,
        in_specs=[smem] * 3 + [vmem] * (len(arrays) + 3),
        out_specs=jax.tree.map(lambda _: vmem, out_shape),
        scratch_shapes=[
            pltpu.VMEM((sources, vectors, leaf), jnp.float32),
            pltpu.VMEM((targets, vectors, leaf), jnp.float32),
        ],
        compiler_params=pltpu.CompilerParams(vmem_limit_bytes=room * 1024 * 1024),
        cost_estimate=pl.CostEstimate(
            flops=2 * leaf * flat * vectors * (sources + targets + blocks.shape[0]),
            bytes_accessed=2 * (2 * flat * leaf + blocks.size),
            transcendentals=0,
        ),
    )(*pairs, *arrays, *[basis.reshape(flat, leaf) for basis in bases], blocks)


def hold_kernel(*refs):
    count = len(refs) // 2
    sems = refs[-1]
    copies = [
        pltpu.make_async_copy(refs[place], refs[count + place], sems.at[place])
        for place in range(count)
    ]
    for copy in copies:
        copy.start()
    for copy in copies:
        copy.wait()


def hold(*arrays):
    anywhere = pl.BlockSpec(memory_space=pl.ANY)
    return pl.pallas_call(
        hold_kernel,
        out_shape=[jax.ShapeDtypeStruct(a.shape, a.dtype) for a in arrays],
        in_specs=[anywhere] * len(arrays),
        out_specs=[anywhere] * len(arrays),
        scratch_shapes=[pltpu.SemaphoreType.DMA((len(arrays),))],
        compiler_params=pltpu.CompilerParams(vmem_limit_bytes=16 * 1024 * 1024),
        cost_estimate=pl.CostEstimate(
            flops=0, bytes_accessed=4 * sum(a.size for a in arrays), transcendentals=0
        ),
    )(*arrays)


def on_device(charges, dense_blocks, dense_index, dense_live, left_basis, right_basis, low_index):
    _, vectors, leaf = charges.shape
    rows = lax.axis_size("col")
    cols = lax.axis_size("row")
    row_line = turned(cols, cols - 2)
    back_line = turned(cols, 4)
    col_line = outward(rows, 10)
    copies = jnp.broadcast_to(charges, (cols, vectors, leaf))
    col_charges = lax.all_to_all(copies, "row", 0, 0, axis_index_groups=[row_line[0]], tiled=True)
    left = left_basis[0, 0]
    right, blocks = hold(right_basis[0, 0], dense_blocks[0, 0])
    dense_pairs = dense_index[0, 0]
    low_pairs = low_index[0, 0]
    mixed = apply_slots(
        forward_kernel, (row_line, col_line), 16,
        (low_pairs, dense_pairs, dense_live),
        (col_charges.reshape(cols * vectors, leaf), charges[0]),
        (right, left), blocks, cols, rows,
        jax.ShapeDtypeStruct((rows, 2 * vectors, leaf), jnp.bfloat16),
    )
    mixed = lax.all_to_all(mixed, "col", 0, 0, axis_index_groups=[col_line[0]], tiled=True)
    col_partial, row_total = apply_slots(
        mirror_kernel, (col_line, back_line), 16,
        (low_pairs, dense_pairs, dense_live),
        (mixed,),
        (left, right), blocks, rows, cols,
        (
            jax.ShapeDtypeStruct((cols * vectors, leaf), jnp.bfloat16),
            jax.ShapeDtypeStruct((vectors, leaf), jnp.float32),
        ),
    )
    col_parts = lax.all_to_all(
        col_partial.reshape(cols, vectors, leaf), "row", 0, 0,
        axis_index_groups=[back_line[0]], tiled=True,
    )
    col_total = jnp.sum(col_parts.astype(jnp.float32), axis=0)
    return (row_total + col_total).astype(jnp.bfloat16)[None]


def solution(mesh):
    in_specs = (
        P(("row", "col"), None, None),
        P("row", "col", None, None, None),
        P("row", "col", None, None),
        P("row", "col"),
        P("row", "col", None, None, None),
        P("row", "col", None, None, None),
        P("row", "col", None, None),
    )
    out_specs = P(("row", "col"), None, None)
    return jax.shard_map(
        on_device, mesh=mesh, in_specs=in_specs, out_specs=out_specs, check_vma=False
    )
```
